1024 devices in a mesh: group: 128 (over z, y), head: 8 (over x, core).
Axes of the slice: x: 4, y: 8, z: 16, core: 2. Of those that a mesh axis runs over, the one named last changes fastest.
Arguments:
- hidden_in: bfloat16 [3, 1024, 4096], P(None, 'group'), may hold values from -6 to 6
- norm_gain: float32 [4096], replicated, may hold values from 0.5 to 1.5
- w_gate_up: bfloat16 [128, 4096, 2, 1024], P('group', 'head'), may hold values from -0.09375 to 0.09375
- w_down: bfloat16 [128, 1024, 4096], P('group', None, 'head'), may hold values from -0.1875 to 0.1875
- route_ids: int32 [3, 1024, 8], P(None, 'group'), may hold values from 0 to 127, as said below
- route_weights: float32 [3, 1024, 8], P(None, 'group'), may hold values from 0.05 to 1
Outputs:
- mixed: bfloat16 [3, 1024, 4096], P(None, 'group', 'head')
The draws below stay inside these ranges and needn't reach their ends.
Inputs may be any that keep to these rules, and one draw needn't show every extreme that they name: `route_ids`: in each micro-batch the 8 rows of one group name 8 different experts each, and no expert is named twice within that group and micro-batch.
All inputs are finite; a program needn't handle non-finite values.
Results may differ from the reference program's by a relative error of at most 0.012.
Values may be sent and summed in bfloat16 or wider, within the bound.
A program may use at most 32 MiB of HBM per device.

```python
import math
import jax
import jax.numpy as jnp
from jax import lax

D = 4096
FF = 1024
TOPK = 8
MB = 3
ROUTED_EXPERTS = 128
ROWS = 8
TOKENS = 1024
N_GROUP = 128
N_HEAD = 8


def draw_route_ids(key, part):
    key = jax.random.fold_in(key, 7)
    popular_key, hottest_key, block_key = jax.random.split(key, 3)
    block_count = MB * (TOKENS // ROWS)
    expert_number = jnp.arange(ROUTED_EXPERTS, dtype=jnp.int32)
    favored_experts = jax.random.randint(popular_key, (ROUTED_EXPERTS,), 0, 4096, dtype=jnp.int32)
    busiest_expert = jax.random.randint(hottest_key, (), 0, ROUTED_EXPERTS, dtype=jnp.int32)
    extra_boost = favored_experts + jnp.where(expert_number == busiest_expert, 1048576, 0).astype(jnp.int32)

    def one_block(block_seed):
        noise_key, order_key = jax.random.split(block_seed)
        random_jitter = jax.random.randint(noise_key, (ROUTED_EXPERTS,), 0, 4096, dtype=jnp.int32)
        expert_logits = (random_jitter + extra_boost) * ROUTED_EXPERTS + expert_number
        ranking = jnp.argsort(-expert_logits)
        picked = ranking[:ROWS * TOPK]
        mixed_order = jax.random.permutation(order_key, ROWS * TOPK)
        return picked[mixed_order].reshape(ROWS, TOPK)
    drawn = jax.vmap(one_block)(jax.random.split(block_key, block_count))
    return drawn.reshape(MB, TOKENS, TOPK).astype(jnp.int32)


def block_scale(own_key, shape, pieces, least, high):
    def one(position, shards_of):
        heights = jax.random.uniform(jax.random.fold_in(jax.random.fold_in(own_key, 6), position), (shards_of,), jnp.float32, least / len(pieces), high / len(pieces))
        return jnp.repeat(jnp.exp(heights), shape[position] // shards_of).reshape((-1,) + (1,) * (len(shape) - position - 1))

    gain = one(*pieces[0])
    for cut in pieces[1:]:
        gain = gain * one(*cut)
    return gain


def noise(own_key, shape, scale, reach, shards=(), held_as=jnp.bfloat16):
    result = jax.random.normal(own_key, shape, jnp.float32) * scale
    if len(shards) > 0:
        result = block_scale(own_key, shape, shards, -0.22, 0.18) * result
    return jnp.clip(result, min=-reach, max=reach).astype(held_as)


def setup_inputs(seed: int = 0) -> dict:
    key_of = jax.random.split(jax.random.key(seed), 7)
    return {
        "hidden_in": noise(key_of[0], (MB, TOKENS, D), 1.0, 6.0, ((1, 128),)),
        "norm_gain": jnp.clip(1.0 + 0.1 * jax.random.normal(key_of[1], (D,), jnp.float32), 0.5, 1.5),
        "w_gate_up": noise(key_of[2], (ROUTED_EXPERTS, D, 2, FF), D ** -0.5, 0.09375, ((0, 128), (1, 8))),
        "w_down": noise(key_of[3], (ROUTED_EXPERTS, FF, D), FF ** -0.5, 0.1875, ((0, 128), (2, 8))),
        "route_ids": draw_route_ids(jax.random.fold_in(key_of[6], 71), 0),
        "route_weights": jnp.clip(jnp.exp(math.log(1.0) - 2.9957323 * jax.random.uniform(key_of[5], (MB, TOKENS, TOPK), jnp.float32) ** block_scale(key_of[5], (MB, TOKENS, TOPK), ((1, 128),), -0.2, 0.2)), 0.05, 1.0),
    }


def one_batch(tokens, chosen_ids, raw_weights, norm_gain, w_gate_up, w_down):
    slice_width = D // N_HEAD
    wide_tokens = tokens.astype(jnp.float32)
    scale = lax.rsqrt(lax.optimization_barrier(jnp.mean(wide_tokens * wide_tokens, axis=-1, keepdims=True)) + 1e-06)
    normed = (wide_tokens * scale * norm_gain.astype(jnp.float32)).astype(jnp.bfloat16)
    gate_probs = raw_weights / lax.optimization_barrier(jnp.sum(raw_weights, axis=-1, keepdims=True))
    blocks = normed.reshape(N_GROUP, ROWS, N_HEAD, slice_width).astype(jnp.float32)
    group_ids = chosen_ids.reshape(N_GROUP, ROWS, TOPK)
    group_gates = gate_probs.reshape(N_GROUP, ROWS, TOPK)

    def add_expert(running, expert):
        matches = group_ids == expert
        chosen = jnp.any(matches, axis=-1).astype(jnp.float32)
        row_gate = lax.optimization_barrier(jnp.sum(jnp.where(matches, group_gates, jnp.float32(0.0)), axis=-1))
        slot_rows = jnp.einsum('gr,grhw->ghw', chosen, blocks).astype(jnp.bfloat16)
        weights_here = w_gate_up[expert].reshape(N_HEAD, slice_width, 2, FF).astype(jnp.float32)
        products = jnp.einsum('ghw,hwcf->hgcf', slot_rows.astype(jnp.float32), weights_here)
        rounded = lax.optimization_barrier(products.astype(jnp.bfloat16))
        summed = lax.optimization_barrier(jnp.sum(rounded.astype(jnp.float32), axis=0))
        activated = (jax.nn.silu(summed[:, 0]) * summed[:, 1]).astype(jnp.bfloat16)
        expert_rows = jnp.dot(activated, w_down[expert], preferred_element_type=jnp.float32).astype(jnp.bfloat16)
        running = running + row_gate[:, :, None] * expert_rows.astype(jnp.float32)[:, None, :]
        return (running, None)
    start_total = jnp.zeros((N_GROUP, ROWS, D), jnp.float32)
    running, unused = lax.scan(add_expert, start_total, jnp.arange(ROUTED_EXPERTS, dtype=jnp.int32))
    return (wide_tokens + running.reshape(TOKENS, D)).astype(jnp.bfloat16)

def reference(hidden_in, norm_gain, w_gate_up, w_down, route_ids, route_weights):
    results = []
    for micro_batch in range(MB):
        results.append(one_batch(hidden_in[micro_batch], route_ids[micro_batch], route_weights[micro_batch], norm_gain, w_gate_up, w_down))
    return jnp.stack(results)
```

```python
import functools

import jax
import jax.numpy as jnp
from jax import lax
from jax.experimental import pallas as pl
from jax.experimental.pallas import tpu as pltpu
from jax.sharding import PartitionSpec as P

MESH = pl.DeviceIdType.MESH
F32 = jnp.float32
BF16 = jnp.bfloat16
NEAR = 4
CORES = 2
META = 16


class Copies:
    def __init__(self, send_sem, recv_sem):
        self.send_sem, self.recv_sem = send_sem, recv_sem
        self.all = []

    def start(self, src, dst, device):
        i = len(self.all)
        copy = pltpu.make_async_remote_copy(
            src_ref=src,
            dst_ref=dst,
            send_sem=self.send_sem.at[i],
            recv_sem=self.recv_sem.at[i],
            device_id=device,
            device_id_type=MESH,
        )
        copy.start()
        self.all.append(copy)
        return copy


def copy_count(dims):
    nz, ny, nx, mb = dims
    far, near, along_y, along_x = nz // NEAR - 1, 4, ny - 1, nx - 1
    return (far + near) + mb * 2 * (far + near + along_y + along_x + 1)


def kernel(
    dims, h_ref, gain_ref, ids_ref, weights_ref, gate_up_hbm, down_hbm, out_ref,
    raw, gate_up, down, meta, meta_t, mixing, rows, slots, arrived, terms, core_in, pair_sum,
    x_in, activated, expert_out, returned, partial, near_in, z_sum, far_in,
    load_sem, send_sem, recv_sem,
):
    nz, ny, nx, mb = dims
    far = nz // NEAR
    head_count = nx * CORES
    width = rows.shape[-1] * 2
    half_width = width // 2
    ff = activated.shape[-1]
    topk = ids_ref.shape[-1]
    group = lax.axis_index("group")
    head = lax.axis_index("head")
    z, y = lax.div(group, ny), lax.rem(group, ny)
    x, core = lax.div(head, CORES), lax.rem(head, CORES)
    residue, block = lax.rem(z, NEAR), lax.div(z, NEAR)
    place = residue * far + block
    share = core * nx + x

    load_gate_up = pltpu.make_async_copy(gate_up_hbm.at[0], raw, load_sem.at[0])
    load_down = pltpu.make_async_copy(down_hbm.at[0], down, load_sem.at[1])
    load_gate_up.start()
    load_down.start()

    def at_z(step):
        return {"group": lax.rem(z + step + nz, nz) * ny + y, "head": head}

    def at_y(other):
        return {"group": z * ny + other, "head": head}

    def at_x(other):
        return {"group": group, "head": other * CORES + core}

    other_core = {"group": group, "head": x * CORES + (1 - core)}
    far_steps = [NEAR * k for k in range(1, far)]
    peers = [at_z(s) for s in far_steps + [1, -1, 2, -2]]
    peers += [at_y(lax.rem(y + k, ny)) for k in range(1, ny)]
    peers += [at_x(lax.rem(x + k, nx)) for k in range(1, nx)]
    peers += [other_core]
    barrier = pltpu.get_barrier_semaphore()
    for peer in peers:
        pl.semaphore_signal(barrier, inc=1, device_id=peer, device_id_type=MESH)

    copies = Copies(send_sem, recv_sem)
    pending = {}

    def landed(name):
        for copy in pending.pop(name):
            copy.wait_recv()

    column = pl.multiple_of(head * width, 128)

    lane = lax.broadcasted_iota(jnp.int32, (8, 128), 1)
    tile = jnp.zeros((8, 128), F32)
    for m in range(mb):
        ids = ids_ref[m].astype(F32)
        raw_weights = weights_ref[m]
        probs = raw_weights / jnp.sum(raw_weights, axis=-1, keepdims=True)
        for k in range(topk):
            tile = jnp.where(lane == META * m + k, ids[:, k : k + 1], tile)
            tile = jnp.where(lane == META * m + 8 + k, probs[:, k : k + 1], tile)
    meta[place] = tile

    def norm(m):
        wide = h_ref[m].astype(F32)
        scale = lax.rsqrt(jnp.mean(wide * wide, axis=-1, keepdims=True) + 1e-06)
        own = h_ref[m, :, pl.ds(column, width)].astype(F32)
        chunks = width // 128
        gain = jnp.concatenate([gain_ref[pl.ds(head * chunks + j, 1), :] for j in range(chunks)], axis=1)
        normed = own * scale * gain
        rows[m, place] = jnp.concatenate([normed[:, :half_width], normed[:, half_width:]], axis=0).astype(BF16)

    def gather_far(m):
        if m == 0:
            pending["meta far"] = [copies.start(meta.at[place], meta.at[place], at_z(s)) for s in far_steps]
        block_ref = rows.at[m, place]
        pending["far", m] = [copies.start(block_ref, block_ref, at_z(s)) for s in far_steps]

    def near_copies(ref):
        whole = ref.at[pl.ds(residue * far, far)]
        low = ref.at[pl.ds(residue * far, far // 2)]
        high = ref.at[pl.ds(residue * far + far // 2, far // 2)]
        return [
            copies.start(part, part, at_z(step)) for part, step in ((whole, 1), (whole, -1), (low, 2), (high, -2))
        ]

    def gather_near(m):
        if m == 0:
            landed("meta far")
            pending["meta near"] = near_copies(meta)
        landed(("far", m))
        pending["near", m] = near_copies(rows.at[m])

    quads = nz * 16
    lane_q = lax.broadcasted_iota(jnp.int32, (nz, quads), 1)
    slot_p = lax.broadcasted_iota(jnp.int32, (nz, quads), 0)
    same_group = slot_p == lax.div(lane_q, 16)
    first_half = lax.rem(lax.div(lax.broadcasted_iota(jnp.int32, (ny * nz, quads), 1), 8), 2) == 0

    def routing(m, values):
        out = []
        ids = meta_t[META * m : META * m + 8, :]
        probs = meta_t[META * m + 8 : META * m + 16, :]
        valid = lax.broadcasted_iota(jnp.int32, ids.shape, 0) < topk
        for other in range(ny):
            match = jnp.logical_and(ids == (z * ny + other).astype(F32), valid)
            picked = jnp.where(match, probs if values else 1.0, 0.0)
            found = jnp.sum(picked, axis=0, keepdims=True)
            out.append(jnp.where(same_group, found, 0.0))
        return jnp.concatenate(out, axis=0)

    def dispatch(m):
        landed(("near", m))
        if m == 0:
            landed("meta near")
            own = meta[...]
            twice = jnp.concatenate([own, own], axis=1).reshape(quads, 128)
            meta_t[...] = twice.T
        chosen = routing(m, False)
        source = rows[m].reshape(quads, half_width)
        for half in range(2):
            pick = jnp.where(first_half if half == 0 else jnp.logical_not(first_half), chosen, 0.0).astype(BF16)
            got = jnp.dot(pick, source, preferred_element_type=F32).astype(BF16)
            slots[m, :, :, half * half_width : (half + 1) * half_width] = got.reshape(ny, nz, half_width)
        pending["y", m] = send_y(slots.at[m], arrived.at[m])
        arrived[m, y] = slots[m, y]

    def send_y(source, target):
        started = []
        for k in range(1, ny):
            other = lax.rem(y + k, ny)
            started.append(copies.start(source.at[other], target.at[y], at_y(other)))
        return started

    def mix_weights(m):
        gates = routing(m, True)
        for half in range(2):
            keep = jnp.where(first_half if half == 0 else jnp.logical_not(first_half), gates, 0.0)
            mixing[m, half] = keep.T.astype(BF16)

    def expert_in(m):
        landed(("y", m))
        block_in = arrived[m].reshape(ny * nz, width)
        step = min(256, ff)
        for part in range(2):
            for start in range(0, ff, step):
                got = jnp.dot(block_in, gate_up[part, :, start : start + step], preferred_element_type=F32)
                at = part * ff + start
                terms[m, :, :, at : at + step] = got.astype(BF16).reshape(ny, nz, step)
        pending["core", m] = [
            copies.start(terms.at[m, pl.ds((1 - core) * nx, nx)], core_in.at[m], other_core)
        ]

    def pair(m):
        landed(("core", m))
        total = terms[m, pl.ds(core * nx, nx)].astype(F32) + core_in[m].astype(F32)
        pair_sum[m] = total.astype(BF16)
        pending["x", m] = []
        for k in range(1, nx):
            other = lax.rem(x + k, nx)
            pending["x", m].append(copies.start(pair_sum.at[m, other], x_in.at[m, k - 1], at_x(other)))

    def activate(m):
        landed(("x", m))
        total = pair_sum[m, x].astype(F32)
        for k in range(nx - 1):
            total = total + x_in[m, k].astype(F32)
        gate, up = total[:, :ff], total[:, ff:]
        activated[m, share] = (gate / (1.0 + jnp.exp(-gate)) * up).astype(BF16)
        own = activated.at[m, share]
        pending["x back", m] = [
            copies.start(own, own, at_x(lax.rem(x + k, nx))) for k in range(1, nx)
        ]

    def share_pair(m):
        landed(("x back", m))
        own = activated.at[m, pl.ds(core * nx, nx)]
        pending["core back", m] = [copies.start(own, own, other_core)]

    def expert_back(m):
        landed(("core back", m))
        got = jnp.dot(activated[m].reshape(ny * nz, ff), down[...], preferred_element_type=F32)
        expert_out[m] = got.astype(BF16).reshape(ny, nz, width)
        pending["y back", m] = send_y(expert_out.at[m], returned.at[m])
        returned[m, y] = expert_out[m, y]

    def mix(m):
        landed(("y back", m))
        back = returned[m].reshape(ny * nz, width)
        got = jnp.dot(mixing[m, 0], back[:, :half_width], preferred_element_type=F32)
        got = got + jnp.dot(mixing[m, 1], back[:, half_width:], preferred_element_type=F32)
        partial[m] = got.astype(BF16).reshape(nz, 16, half_width)
        source = partial.at[m]

        def of(cls, first, count):
            return source.at[pl.ds(lax.rem(residue + cls, NEAR) * far + first, count)]

        pending["near back", m] = [
            copies.start(of(1, 0, far), near_in.at[m, 0], at_z(1)),
            copies.start(of(3, 0, far), near_in.at[m, 1], at_z(-1)),
            copies.start(of(2, 0, far // 2), near_in.at[m, 2, pl.ds(0, far // 2)], at_z(2)),
            copies.start(of(2, far // 2, far // 2), near_in.at[m, 2, pl.ds(far // 2, far // 2)], at_z(-2)),
        ]

    def reduce_near(m):
        landed(("near back", m))
        total = partial[m, pl.ds(residue * far, far)].astype(F32)
        for k in range(3):
            total = total + near_in[m, k].astype(F32)
        z_sum[m] = total.astype(BF16)
        pending["far back", m] = []
        for k in range(1, far):
            other = lax.rem(block + k, far)
            pending["far back", m].append(
                copies.start(z_sum.at[m, other], far_in.at[m, k - 1], at_z(NEAR * k))
            )

    def finish(m):
        landed(("far back", m))
        total = z_sum[m, block].astype(F32)
        for k in range(far - 1):
            total = total + far_in[m, k].astype(F32)
        residual = h_ref[m, :, pl.ds(column, width)].astype(F32)
        out_ref[m, :, :half_width] = (residual[:, :half_width] + total[:8]).astype(BF16)
        out_ref[m, :, half_width:] = (residual[:, half_width:] + total[8:]).astype(BF16)

    step = 16
    steps = width // step

    def unpack(first, last):
        def body(i, carry):
            at = pl.ds(pl.multiple_of(i * step, step), step)
            both = raw[at].astype(F32)
            gate_up[0, at, :] = both[:, 0, :].astype(BF16)
            gate_up[1, at, :] = both[:, 1, :].astype(BF16)
            return carry

        lax.fori_loop(first, last, body, 0)

    batches = range(mb)
    for m in batches:
        norm(m)
        if m == 0:
            pl.semaphore_wait(barrier, len(peers))
        gather_far(m)
    load_gate_up.wait()
    unpack(0, steps // 4)
    for m in batches:
        gather_near(m)
    unpack(steps // 4, steps // 2)
    for m in batches:
        dispatch(m)
    unpack(steps // 2, steps)
    load_down.wait()
    for m in batches:
        expert_in(m)
    for m in batches:
        mix_weights(m)
    for stage in (pair, activate, share_pair, expert_back, mix, reduce_near, finish):
        for m in batches:
            stage(m)
    for copy in copies.all:
        copy.wait_send()


def per_device(dims, hidden_in, norm_gain, w_gate_up, w_down, route_ids, route_weights):
    nz, ny, nx, mb = dims
    far = nz // NEAR
    width, ff = w_gate_up.shape[1], w_gate_up.shape[3]
    vmem = pl.BlockSpec(memory_space=pltpu.VMEM)
    hbm = pl.BlockSpec(memory_space=pl.ANY)
    count = copy_count(dims)
    scratch = [
        pltpu.VMEM((width, 2, ff), BF16),
        pltpu.VMEM((2, width, ff), BF16),
        pltpu.VMEM((ff, width), BF16),
        pltpu.VMEM((nz, 8, 128), F32),
        pltpu.VMEM((128, nz * 16), F32),
        pltpu.VMEM((mb, 2, nz * 16, ny * nz), BF16),
        pltpu.VMEM((mb, nz, 16, width // 2), BF16),
        pltpu.VMEM((mb, ny, nz, width), BF16),
        pltpu.VMEM((mb, ny, nz, width), BF16),
        pltpu.VMEM((mb, ny, nz, 2 * ff), BF16),
        pltpu.VMEM((mb, nx, nz, 2 * ff), BF16),
        pltpu.VMEM((mb, nx, nz, 2 * ff), BF16),
        pltpu.VMEM((mb, max(nx - 1, 1), nz, 2 * ff), BF16),
        pltpu.VMEM((mb, ny, nz, ff), BF16),
        pltpu.VMEM((mb, ny, nz, width), BF16),
        pltpu.VMEM((mb, ny, nz, width), BF16),
        pltpu.VMEM((mb, nz, 16, width // 2), BF16),
        pltpu.VMEM((mb, 3, far, 16, width // 2), BF16),
        pltpu.VMEM((mb, far, 16, width // 2), BF16),
        pltpu.VMEM((mb, far - 1, 16, width // 2), BF16),
        pltpu.SemaphoreType.DMA((2,)),
        pltpu.SemaphoreType.DMA((count,)),
        pltpu.SemaphoreType.DMA((count,)),
    ]
    return pl.pallas_call(
        functools.partial(kernel, dims),
        out_shape=jax.ShapeDtypeStruct((mb, hidden_in.shape[1], width), BF16),
        in_specs=[vmem, vmem, vmem, vmem, hbm, hbm],
        out_specs=vmem,
        scratch_shapes=scratch,
        compiler_params=pltpu.CompilerParams(
            collective_id=0, has_side_effects=True, vmem_limit_bytes=44 << 20
        ),
    )(hidden_in, norm_gain.reshape(-1, 128), route_ids, route_weights, w_gate_up, w_down)


def solution(mesh, ny=8):
    group_count, head_count = mesh.shape["group"], mesh.shape["head"]

    def run(hidden_in, norm_gain, w_gate_up, w_down, route_ids, route_weights):
        dims = (group_count // ny, ny, head_count // CORES, hidden_in.shape[0])
        return jax.shard_map(
            functools.partial(per_device, dims),
            mesh=mesh,
            in_specs=(
                P(None, "group", None),
                P(),
                P("group", "head", None, None),
                P("group", None, "head"),
                P(None, "group", None),
                P(None, "group", None),
            ),
            out_specs=P(None, "group", "head"),
            check_vma=False,
        )(hidden_in, norm_gain, w_gate_up, w_down, route_ids, route_weights)

    return run
```

```python
import functools

import jax
import jax.numpy as jnp
from jax import lax
from jax.experimental import pallas as pl
from jax.experimental.pallas import tpu as pltpu
from jax.sharding import PartitionSpec as P

MESH = pl.DeviceIdType.MESH
F32 = jnp.float32
BF16 = jnp.bfloat16
NEAR = 2
CORES = 2
META = 16


class Copies:
    def __init__(self, send_sem, recv_sem):
        self.send_sem, self.recv_sem = send_sem, recv_sem
        self.all = []

    def start(self, src, dst, device):
        i = len(self.all)
        copy = pltpu.make_async_remote_copy(
            src_ref=src,
            dst_ref=dst,
            send_sem=self.send_sem.at[i],
            recv_sem=self.recv_sem.at[i],
            device_id=device,
            device_id_type=MESH,
        )
        copy.start()
        self.all.append(copy)
        return copy


def copy_count(dims):
    nz, ny, nx, mb = dims
    far, to_slots = nz // NEAR - 1, NEAR * ny - 1
    return far + mb * 2 * (far + to_slots + (nx - 1) + 1)


def kernel(
    dims, h_hbm, gain_hbm, ids_hbm, weights_hbm, gate_up_hbm, down_hbm, out_ref,
    h_ref, gain_ref, ids_ref, weights_ref, raw, gate_up, down, meta, meta_t, mixing, rows, slots, arrived, terms, core_in, pair_sum,
    x_in, activated, expert_out, returned, partial, far_in,
    load_sem, send_sem, recv_sem,
):
    nz, ny, nx, mb = dims
    far = nz // NEAR
    head_count = nx * CORES
    width = rows.shape[-1] * 2
    half_width = width // 2
    ff = activated.shape[-1]
    topk = ids_ref.shape[-1]
    group = lax.axis_index("group")
    head = lax.axis_index("head")
    z, y = lax.div(group, ny), lax.rem(group, ny)
    x, core = lax.div(head, CORES), lax.rem(head, CORES)
    block = lax.div(z, NEAR)
    toward = 1 - 2 * core
    share = core * nx + x

    load_gate_up = pltpu.make_async_copy(gate_up_hbm.at[0], raw, load_sem.at[0])
    load_down = pltpu.make_async_copy(down_hbm.at[0], down, load_sem.at[1])
    load_small = [
        pltpu.make_async_copy(source, target, load_sem.at[2 + i])
        for i, (source, target) in enumerate(
            ((ids_hbm, ids_ref), (weights_hbm, weights_ref), (gain_hbm, gain_ref), (h_hbm, h_ref))
        )
    ]
    for load in load_small:
        load.start()
    load_gate_up.start()
    load_down.start()

    def at_z(step):
        return {"group": lax.rem(z + step + nz, nz) * ny + y, "head": head}

    def at_zy(step, other):
        return {"group": lax.rem(z + step + nz, nz) * ny + other, "head": head}

    def at_x(other):
        return {"group": group, "head": other * CORES + core}

    other_core = {"group": group, "head": x * CORES + (1 - core)}
    far_order = sorted(range(1, far), key=lambda k: -min(k, far - k))
    y_order = sorted(range(1, ny), key=lambda k: -min(k, ny - k))
    others_y = [lax.rem(y + k, ny) for k in y_order] + [y]
    peers = [at_z(NEAR * k) for k in far_order]
    peers += [at_zy(0, other) for other in others_y[:-1]]
    peers += [at_zy(side, other) for side in (1, -1) for other in others_y]
    peers += [at_x(lax.rem(x + k, nx)) for k in range(1, nx)]
    peers += [other_core]
    barrier = pltpu.get_barrier_semaphore()
    for peer in peers:
        pl.semaphore_signal(barrier, inc=1, device_id=peer, device_id_type=MESH)

    copies = Copies(send_sem, recv_sem)
    pending = {}

    def landed(name):
        for copy in pending.pop(name):
            copy.wait_recv()

    column = pl.multiple_of(head * width, 128)
    for load in load_small:
        load.wait()

    lane = lax.broadcasted_iota(jnp.int32, (8, 128), 1)
    tile = jnp.zeros((8, 128), F32)
    for m in range(mb):
        ids = ids_ref[m].astype(F32)
        raw_weights = weights_ref[m]
        probs = raw_weights / jnp.sum(raw_weights, axis=-1, keepdims=True)
        for k in range(topk):
            tile = jnp.where(lane == META * m + k, ids[:, k : k + 1], tile)
            tile = jnp.where(lane == META * m + 8 + k, probs[:, k : k + 1], tile)
    meta[block] = tile

    def norm(m):
        wide = h_ref[m].astype(F32)
        scale = lax.rsqrt(jnp.mean(wide * wide, axis=-1, keepdims=True) + 1e-06)
        own = h_ref[m, :, pl.ds(column, width)].astype(F32)
        chunks = width // 128
        gain = jnp.concatenate([gain_ref[pl.ds(head * chunks + j, 1), :] for j in range(chunks)], axis=1)
        normed = own * scale * gain
        rows[m, block] = jnp.concatenate([normed[:, :half_width], normed[:, half_width:]], axis=0).astype(BF16)

    def gather(m):
        if m == 0:
            own = meta.at[block]
            pending["meta"] = [copies.start(own, own, at_z(NEAR * k)) for k in far_order]
        own_rows = rows.at[m, block]
        pending["far", m] = [copies.start(own_rows, own_rows, at_z(NEAR * k)) for k in far_order]

    quads = far * 16
    lane_q = lax.broadcasted_iota(jnp.int32, (2 * far, quads), 1)
    slot_row = lax.broadcasted_iota(jnp.int32, (2 * far, quads), 0)
    same_block = lax.rem(slot_row, far) == lax.div(lane_q, 16)
    same_half = lax.div(slot_row, far) == lax.rem(lax.div(lane_q, 8), 2)
    same = jnp.logical_and(same_block, same_half)

    def routing(m, values):
        out = []
        ids = meta_t[META * m : META * m + 8, :]
        probs = meta_t[META * m + 8 : META * m + 16, :]
        valid = lax.broadcasted_iota(jnp.int32, ids.shape, 0) < topk
        for side in range(NEAR):
            first = lax.rem(z + toward * side + nz, nz) * ny
            for other in range(ny):
                match = jnp.logical_and(ids == (first + other).astype(F32), valid)
                picked = jnp.where(match, probs if values else 1.0, 0.0)
                found = jnp.sum(picked, axis=0, keepdims=True)
                out.append(jnp.where(same, found, 0.0))
        return jnp.concatenate(out, axis=0)

    def dispatch(m):
        if m == 0:
            landed("meta")
            own = meta[...]
            twice = jnp.concatenate([own, own], axis=1).reshape(quads, 128)
            meta_t[...] = twice.T
        pick = routing(m, False).astype(BF16)
        landed(("far", m))
        got = jnp.dot(pick, rows[m].reshape(quads, half_width), preferred_element_type=F32)
        slots[m] = got.astype(BF16).reshape(NEAR, ny, 2 * far, half_width)
        pending["slots", m] = exchange(slots.at[m], arrived.at[m], toward)
        arrived[m, 0, y] = slots[m, 0, y]

    def exchange(source, target, direction):
        started = []
        for i, other in enumerate(others_y):
            for side in (1, 0):
                if side == 1 or i < ny - 1:
                    device = at_zy(direction * side, other)
                    started.append(copies.start(source.at[side, other], target.at[side, y], device))
        return started

    def mix_weights(m):
        mixing[m] = routing(m, True).T.astype(BF16)

    def expert_in(m):
        landed(("slots", m))
        folded = arrived[m].astype(F32).reshape(NEAR * ny, 2 * far, half_width)
        halves = [folded[:, h * far : (h + 1) * far].reshape(ny * nz, half_width) for h in range(2)]
        block_in = jnp.concatenate(halves, axis=1).astype(BF16)
        step = min(256, ff)
        for part in range(2):
            for start in range(0, ff, step):
                got = jnp.dot(block_in, gate_up[part, :, start : start + step], preferred_element_type=F32)
                at = part * ff + start
                terms[m, :, :, at : at + step] = got.astype(BF16).reshape(ny, nz, step)
        pending["core", m] = [
            copies.start(terms.at[m, pl.ds((1 - core) * nx, nx)], core_in.at[m], other_core)
        ]

    def pair(m):
        landed(("core", m))
        total = terms[m, pl.ds(core * nx, nx)].astype(F32) + core_in[m].astype(F32)
        pair_sum[m] = total.astype(BF16)
        pending["x", m] = []
        for k in range(1, nx):
            other = lax.rem(x + k, nx)
            pending["x", m].append(copies.start(pair_sum.at[m, other], x_in.at[m, k - 1], at_x(other)))

    def activate(m):
        landed(("x", m))
        total = pair_sum[m, x].astype(F32)
        for k in range(nx - 1):
            total = total + x_in[m, k].astype(F32)
        gate, up = total[:, :ff], total[:, ff:]
        activated[m, share] = (gate / (1.0 + jnp.exp(-gate)) * up).astype(BF16)
        own = activated.at[m, share]
        pending["x back", m] = [
            copies.start(own, own, at_x(lax.rem(x + k, nx))) for k in range(1, nx)
        ]

    def share_pair(m):
        landed(("x back", m))
        own = activated.at[m, pl.ds(core * nx, nx)]
        pending["core back", m] = [copies.start(own, own, other_core)]

    def expert_back(m):
        landed(("core back", m))
        got = jnp.dot(activated[m].reshape(ny * nz, ff), down[...], preferred_element_type=F32)
        got = got.reshape(NEAR * ny, far, width)
        folded = jnp.concatenate([got[:, :, :half_width], got[:, :, half_width:]], axis=1)
        expert_out[m] = folded.astype(BF16).reshape(NEAR, ny, 2 * far, half_width)
        pending["slots back", m] = exchange(expert_out.at[m], returned.at[m], -toward)
        returned[m, 0, y] = expert_out[m, 0, y]

    def mix(m):
        landed(("slots back", m))
        back = returned[m].reshape(NEAR * ny * 2 * far, half_width)
        got = jnp.dot(mixing[m], back, preferred_element_type=F32)
        partial[m] = got.astype(BF16).reshape(far, 16, half_width)
        pending["far back", m] = []
        for k in far_order:
            other = lax.rem(block + k, far)
            pending["far back", m].append(
                copies.start(partial.at[m, other], far_in.at[m, k - 1], at_z(NEAR * k))
            )

    def finish(m):
        landed(("far back", m))
        total = partial[m, block].astype(F32)
        for k in range(far - 1):
            total = total + far_in[m, k].astype(F32)
        residual = h_ref[m, :, pl.ds(column, width)].astype(F32)
        out_ref[m, :, :half_width] = (residual[:, :half_width] + total[:8]).astype(BF16)
        out_ref[m, :, half_width:] = (residual[:, half_width:] + total[8:]).astype(BF16)

    step = 16
    steps = width // step

    def unpack():
        def body(i, carry):
            at = pl.ds(pl.multiple_of(i * step, step), step)
            both = raw[at].astype(F32)
            gate_up[0, at, :] = both[:, 0, :].astype(BF16)
            gate_up[1, at, :] = both[:, 1, :].astype(BF16)
            return carry

        lax.fori_loop(0, steps, body, 0)

    batches = range(mb)
    for m in batches:
        norm(m)
        if m == 0:
            pl.semaphore_wait(barrier, len(peers))
        gather(m)
    load_gate_up.wait()
    unpack()
    load_down.wait()
    for m in batches:
        dispatch(m)
    for m in batches:
        mix_weights(m)
    due = ((expert_in, 15), (pair, 17.5), (activate, 22), (share_pair, 26), (expert_back, 27.5), (mix, 32), (finish, 38))
    order = sorted((at + 3 * m, m, i) for i, (_, at) in enumerate(due) for m in batches)
    for _, m, i in order:
        due[i][0](m)
    for copy in copies.all:
        copy.wait_send()


def per_device(dims, hidden_in, norm_gain, w_gate_up, w_down, route_ids, route_weights):
    nz, ny, nx, mb = dims
    far = nz // NEAR
    width, ff = w_gate_up.shape[1], w_gate_up.shape[3]
    vmem = pl.BlockSpec(memory_space=pltpu.VMEM)
    hbm = pl.BlockSpec(memory_space=pltpu.HBM)
    count = copy_count(dims)
    gain = norm_gain.reshape(-1, 128)
    scratch = [
        *(pltpu.VMEM(a.shape, a.dtype) for a in (hidden_in, gain, route_ids, route_weights)),
        pltpu.VMEM((width, 2, ff), BF16),
        pltpu.VMEM((2, width, ff), BF16),
        pltpu.VMEM((ff, width), BF16),
        pltpu.VMEM((far, 8, 128), F32),
        pltpu.VMEM((128, far * 16), F32),
        pltpu.VMEM((mb, far * 16, NEAR * ny * 2 * far), BF16),
        pltpu.VMEM((mb, far, 16, width // 2), BF16),
        pltpu.VMEM((mb, NEAR, ny, 2 * far, width // 2), BF16),
        pltpu.VMEM((mb, NEAR, ny, 2 * far, width // 2), BF16),
        pltpu.VMEM((mb, ny, nz, 2 * ff), BF16),
        pltpu.VMEM((mb, nx, nz, 2 * ff), BF16),
        pltpu.VMEM((mb, nx, nz, 2 * ff), BF16),
        pltpu.VMEM((mb, max(nx - 1, 1), nz, 2 * ff), BF16),
        pltpu.VMEM((mb, ny, nz, ff), BF16),
        pltpu.VMEM((mb, NEAR, ny, 2 * far, width // 2), BF16),
        pltpu.VMEM((mb, NEAR, ny, 2 * far, width // 2), BF16),
        pltpu.VMEM((mb, far, 16, width // 2), BF16),
        pltpu.VMEM((mb, far - 1, 16, width // 2), BF16),
        pltpu.SemaphoreType.DMA((6,)),
        pltpu.SemaphoreType.DMA((count,)),
        pltpu.SemaphoreType.DMA((count,)),
    ]
    return pl.pallas_call(
        functools.partial(kernel, dims),
        out_shape=jax.ShapeDtypeStruct((mb, hidden_in.shape[1], width), BF16),
        in_specs=[hbm] * 6,
        out_specs=vmem,
        scratch_shapes=scratch,
        compiler_params=pltpu.CompilerParams(
            collective_id=0, has_side_effects=True, vmem_limit_bytes=60 << 20
        ),
    )(hidden_in, gain, route_ids, route_weights, w_gate_up, w_down)


def solution(mesh, ny=8):
    group_count, head_count = mesh.shape["group"], mesh.shape["head"]

    def run(hidden_in, norm_gain, w_gate_up, w_down, route_ids, route_weights):
        dims = (group_count // ny, ny, head_count // CORES, hidden_in.shape[0])
        return jax.shard_map(
            functools.partial(per_device, dims),
            mesh=mesh,
            in_specs=(
                P(None, "group", None),
                P(),
                P("group", "head", None, None),
                P("group", None, "head"),
                P(None, "group", None),
                P(None, "group", None),
            ),
            out_specs=P(None, "group", "head"),
            check_vma=False,
        )(hidden_in, norm_gain, w_gate_up, w_down, route_ids, route_weights)

    return run
```

```python
import functools

import jax
import jax.numpy as jnp
from jax import lax
from jax.experimental import pallas as pl
from jax.experimental.pallas import tpu as pltpu
from jax.sharding import PartitionSpec as P

MESH = pl.DeviceIdType.MESH
F32 = jnp.float32
BF16 = jnp.bfloat16
NEAR = 2
CORES = 2
META = 16


class Copies:
    def __init__(self, send_sem, recv_sem):
        self.send_sem, self.recv_sem = send_sem, recv_sem
        self.all = []

    def start(self, src, dst, device):
        i = len(self.all)
        copy = pltpu.make_async_remote_copy(
            src_ref=src,
            dst_ref=dst,
            send_sem=self.send_sem.at[i],
            recv_sem=self.recv_sem.at[i],
            device_id=device,
            device_id_type=MESH,
        )
        copy.start()
        self.all.append(copy)
        return copy


def copy_count(dims):
    nz, ny, nx, mb = dims
    far, to_slots = nz // NEAR - 1, NEAR * ny - 1
    return far + mb * 2 * (far + to_slots + (nx - 1) + 1)


def kernel(
    dims, h_hbm, gain_hbm, ids_hbm, weights_hbm, gate_up_hbm, down_hbm, out_ref,
    h_ref, gain_ref, ids_ref, weights_ref, raw, gate_up, down, meta, meta_t, mixing, rows, slots, arrived, terms, core_in, pair_sum,
    x_in, activated, expert_out, returned, partial, far_in,
    load_sem, send_sem, recv_sem,
):
    nz, ny, nx, mb = dims
    far = nz // NEAR
    head_count = nx * CORES
    width = rows.shape[-1] * 2
    half_width = width // 2
    ff = activated.shape[-1]
    topk = ids_ref.shape[-1]
    group = lax.axis_index("group")
    head = lax.axis_index("head")
    z, y = lax.div(group, ny), lax.rem(group, ny)
    x, core = lax.div(head, CORES), lax.rem(head, CORES)
    block = lax.div(z, NEAR)
    toward = 1 - 2 * core
    share = core * nx + x

    load_gate_up = pltpu.make_async_copy(gate_up_hbm.at[0], raw, load_sem.at[0])
    load_down = pltpu.make_async_copy(down_hbm.at[0], down, load_sem.at[1])
    load_small = [
        pltpu.make_async_copy(source, target, load_sem.at[2 + i])
        for i, (source, target) in enumerate(
            ((ids_hbm, ids_ref), (weights_hbm, weights_ref), (gain_hbm, gain_ref), (h_hbm, h_ref))
        )
    ]
    for load in load_small:
        load.start()
    load_gate_up.start()
    load_down.start()

    def at_z(step):
        return {"group": lax.rem(z + step + nz, nz) * ny + y, "head": head}

    def at_zy(step, other):
        return {"group": lax.rem(z + step + nz, nz) * ny + other, "head": head}

    def at_x(other):
        return {"group": group, "head": other * CORES + core}

    other_core = {"group": group, "head": x * CORES + (1 - core)}
    far_order = sorted(range(1, far), key=lambda k: -min(k, far - k))
    y_order = sorted(range(1, ny), key=lambda k: -min(k, ny - k))
    others_y = [lax.rem(y + k, ny) for k in y_order] + [y]
    peers = [at_z(NEAR * k) for k in far_order]
    peers += [at_zy(0, other) for other in others_y[:-1]]
    peers += [at_zy(side, other) for side in (1, -1) for other in others_y]
    peers += [at_x(lax.rem(x + k, nx)) for k in range(1, nx)]
    peers += [other_core]
    barrier = pltpu.get_barrier_semaphore()
    for peer in peers:
        pl.semaphore_signal(barrier, inc=1, device_id=peer, device_id_type=MESH)

    copies = Copies(send_sem, recv_sem)
    pending = {}

    def landed(name):
        for copy in pending.pop(name):
            copy.wait_recv()

    column = pl.multiple_of(head * width, 128)
    for load in load_small:
        load.wait()

    lane = lax.broadcasted_iota(jnp.int32, (8, 128), 1)
    tile = jnp.zeros((8, 128), F32)
    for m in range(mb):
        ids = ids_ref[m].astype(F32)
        raw_weights = weights_ref[m]
        probs = raw_weights / jnp.sum(raw_weights, axis=-1, keepdims=True)
        for k in range(topk):
            tile = jnp.where(lane == META * m + k, ids[:, k : k + 1], tile)
            tile = jnp.where(lane == META * m + 8 + k, probs[:, k : k + 1], tile)
    meta[block] = tile

    def norm(m):
        wide = h_ref[m].astype(F32)
        scale = lax.rsqrt(jnp.mean(wide * wide, axis=-1, keepdims=True) + 1e-06)
        own = h_ref[m, :, pl.ds(column, width)].astype(F32)
        chunks = width // 128
        gain = jnp.concatenate([gain_ref[pl.ds(head * chunks + j, 1), :] for j in range(chunks)], axis=1)
        normed = own * scale * gain
        rows[m, block] = jnp.concatenate([normed[:, :half_width], normed[:, half_width:]], axis=0).astype(BF16)

    def gather(m):
        if m == 0:
            own = meta.at[block]
            pending["meta"] = [copies.start(own, own, at_z(NEAR * k)) for k in far_order]
        own_rows = rows.at[m, block]
        pending["far", m] = [copies.start(own_rows, own_rows, at_z(NEAR * k)) for k in far_order]

    quads = far * 16
    lane_q = lax.broadcasted_iota(jnp.int32, (2 * far, quads), 1)
    slot_row = lax.broadcasted_iota(jnp.int32, (2 * far, quads), 0)
    same_block = lax.rem(slot_row, far) == lax.div(lane_q, 16)
    same_half = lax.div(slot_row, far) == lax.rem(lax.div(lane_q, 8), 2)
    same = jnp.logical_and(same_block, same_half)

    def routing(m, values):
        out = []
        ids = meta_t[META * m : META * m + 8, :]
        probs = meta_t[META * m + 8 : META * m + 16, :]
        valid = lax.broadcasted_iota(jnp.int32, ids.shape, 0) < topk
        for side in range(NEAR):
            first = lax.rem(z + toward * side + nz, nz) * ny
            for other in range(ny):
                match = jnp.logical_and(ids == (first + other).astype(F32), valid)
                picked = jnp.where(match, probs if values else 1.0, 0.0)
                found = jnp.sum(picked, axis=0, keepdims=True)
                out.append(jnp.where(same, found, 0.0))
        return jnp.concatenate(out, axis=0)

    def dispatch(m):
        if m == 0:
            landed("meta")
            own = meta[...]
            twice = jnp.concatenate([own, own], axis=1).reshape(quads, 128)
            meta_t[...] = twice.T
        pick = routing(m, False).astype(BF16)
        landed(("far", m))
        got = jnp.dot(pick, rows[m].reshape(quads, half_width), preferred_element_type=F32)
        slots[m] = got.astype(BF16).reshape(NEAR, ny, 2 * far, half_width)
        pending["slots", m] = exchange(slots.at[m], arrived.at[m], toward)
        arrived[m, 0, y] = slots[m, 0, y]

    def exchange(source, target, direction):
        started = []
        for i, other in enumerate(others_y):
            for side in (1, 0):
                if side == 1 or i < ny - 1:
                    device = at_zy(direction * side, other)
                    started.append(copies.start(source.at[side, other], target.at[side, y], device))
        return started

    def mix_weights(m):
        mixing[m] = routing(m, True).T.astype(BF16)

    def expert_in(m):
        landed(("slots", m))
        folded = arrived[m].astype(F32).reshape(NEAR * ny, 2 * far, half_width)
        halves = [folded[:, h * far : (h + 1) * far].reshape(ny * nz, half_width) for h in range(2)]
        block_in = jnp.concatenate(halves, axis=1).astype(BF16)
        step = min(256, ff)
        for part in range(2):
            for start in range(0, ff, step):
                got = jnp.dot(block_in, gate_up[part, :, start : start + step], preferred_element_type=F32)
                at = part * ff + start
                terms[m, :, :, at : at + step] = got.astype(BF16).reshape(ny, nz, step)
        pending["core", m] = [
            copies.start(terms.at[m, pl.ds((1 - core) * nx, nx)], core_in.at[m], other_core)
        ]

    def pair(m):
        landed(("core", m))
        total = terms[m, pl.ds(core * nx, nx)].astype(F32) + core_in[m].astype(F32)
        pair_sum[m] = total.astype(BF16)
        pending["x", m] = []
        for k in range(1, nx):
            other = lax.rem(x + k, nx)
            pending["x", m].append(copies.start(pair_sum.at[m, other], x_in.at[m, k - 1], at_x(other)))

    def activate(m):
        landed(("x", m))
        total = pair_sum[m, x].astype(F32)
        for k in range(nx - 1):
            total = total + x_in[m, k].astype(F32)
        gate, up = total[:, :ff], total[:, ff:]
        activated[m, share] = (gate / (1.0 + jnp.exp(-gate)) * up).astype(BF16)
        own = activated.at[m, share]
        pending["x back", m] = [
            copies.start(own, own, at_x(lax.rem(x + k, nx))) for k in range(1, nx)
        ]

    def share_pair(m):
        landed(("x back", m))
        own = activated.at[m, pl.ds(core * nx, nx)]
        pending["core back", m] = [copies.start(own, own, other_core)]

    def expert_back(m):
        landed(("core back", m))
        got = jnp.dot(activated[m].reshape(ny * nz, ff), down[...], preferred_element_type=F32)
        got = got.reshape(NEAR * ny, far, width)
        folded = jnp.concatenate([got[:, :, :half_width], got[:, :, half_width:]], axis=1)
        expert_out[m] = folded.astype(BF16).reshape(NEAR, ny, 2 * far, half_width)
        pending["slots back", m] = exchange(expert_out.at[m], returned.at[m], -toward)
        returned[m, 0, y] = expert_out[m, 0, y]

    def mix(m):
        landed(("slots back", m))
        back = returned[m].reshape(NEAR * ny * 2 * far, half_width)
        got = jnp.dot(mixing[m], back, preferred_element_type=F32)
        partial[m] = got.astype(BF16).reshape(far, 16, half_width)
        pending["far back", m] = []
        for k in far_order:
            other = lax.rem(block + k, far)
            pending["far back", m].append(
                copies.start(partial.at[m, other], far_in.at[m, k - 1], at_z(NEAR * k))
            )

    def finish(m):
        landed(("far back", m))
        total = partial[m, block].astype(F32)
        for k in range(far - 1):
            total = total + far_in[m, k].astype(F32)
        residual = h_ref[m, :, pl.ds(column, width)].astype(F32)
        out_ref[m, :, :half_width] = (residual[:, :half_width] + total[:8]).astype(BF16)
        out_ref[m, :, half_width:] = (residual[:, half_width:] + total[8:]).astype(BF16)

    step = 16
    steps = width // step

    def unpack():
        def body(i, carry):
            at = pl.ds(pl.multiple_of(i * step, step), step)
            both = raw[at].astype(F32)
            gate_up[0, at, :] = both[:, 0, :].astype(BF16)
            gate_up[1, at, :] = both[:, 1, :].astype(BF16)
            return carry

        lax.fori_loop(0, steps, body, 0)

    batches = range(mb)
    for m in batches:
        norm(m)
    pl.semaphore_wait(barrier, len(peers))
    for m in batches:
        gather(m)
    load_gate_up.wait()
    unpack()
    load_down.wait()
    for m in batches:
        dispatch(m)
    for m in batches:
        mix_weights(m)
    due = ((expert_in, 15), (pair, 17.5), (activate, 22), (share_pair, 26), (expert_back, 27.5), (mix, 32), (finish, 38))
    order = sorted((at + 3 * m, m, i) for i, (_, at) in enumerate(due) for m in batches)
    for _, m, i in order:
        due[i][0](m)
    for copy in copies.all:
        copy.wait_send()


def per_device(dims, hidden_in, norm_gain, w_gate_up, w_down, route_ids, route_weights):
    nz, ny, nx, mb = dims
    far = nz // NEAR
    width, ff = w_gate_up.shape[1], w_gate_up.shape[3]
    vmem = pl.BlockSpec(memory_space=pltpu.VMEM)
    hbm = pl.BlockSpec(memory_space=pltpu.HBM)
    count = copy_count(dims)
    gain = norm_gain.reshape(-1, 128)
    scratch = [
        *(pltpu.VMEM(a.shape, a.dtype) for a in (hidden_in, gain, route_ids, route_weights)),
        pltpu.VMEM((width, 2, ff), BF16),
        pltpu.VMEM((2, width, ff), BF16),
        pltpu.VMEM((ff, width), BF16),
        pltpu.VMEM((far, 8, 128), F32),
        pltpu.VMEM((128, far * 16), F32),
        pltpu.VMEM((mb, far * 16, NEAR * ny * 2 * far), BF16),
        pltpu.VMEM((mb, far, 16, width // 2), BF16),
        pltpu.VMEM((mb, NEAR, ny, 2 * far, width // 2), BF16),
        pltpu.VMEM((mb, NEAR, ny, 2 * far, width // 2), BF16),
        pltpu.VMEM((mb, ny, nz, 2 * ff), BF16),
        pltpu.VMEM((mb, nx, nz, 2 * ff), BF16),
        pltpu.VMEM((mb, nx, nz, 2 * ff), BF16),
        pltpu.VMEM((mb, max(nx - 1, 1), nz, 2 * ff), BF16),
        pltpu.VMEM((mb, ny, nz, ff), BF16),
        pltpu.VMEM((mb, NEAR, ny, 2 * far, width // 2), BF16),
        pltpu.VMEM((mb, NEAR, ny, 2 * far, width // 2), BF16),
        pltpu.VMEM((mb, far, 16, width // 2), BF16),
        pltpu.VMEM((mb, far - 1, 16, width // 2), BF16),
        pltpu.SemaphoreType.DMA((6,)),
        pltpu.SemaphoreType.DMA((count,)),
        pltpu.SemaphoreType.DMA((count,)),
    ]
    return pl.pallas_call(
        functools.partial(kernel, dims),
        out_shape=pltpu.VMEM((mb, hidden_in.shape[1], width), BF16),
        in_specs=[hbm] * 6,
        out_specs=vmem,
        scratch_shapes=scratch,
        compiler_params=pltpu.CompilerParams(
            collective_id=0, has_side_effects=True, vmem_limit_bytes=60 << 20
        ),
    )(hidden_in, gain, route_ids, route_weights, w_gate_up, w_down)


def solution(mesh, ny=8):
    group_count, head_count = mesh.shape["group"], mesh.shape["head"]

    def run(hidden_in, norm_gain, w_gate_up, w_down, route_ids, route_weights):
        dims = (group_count // ny, ny, head_count // CORES, hidden_in.shape[0])
        return jax.shard_map(
            functools.partial(per_device, dims),
            mesh=mesh,
            in_specs=(
                P(None, "group", None),
                P(),
                P("group", "head", None, None),
                P("group", None, "head"),
                P(None, "group", None),
                P(None, "group", None),
            ),
            out_specs=P(None, "group", "head"),
            check_vma=False,
        )(hidden_in, norm_gain, w_gate_up, w_down, route_ids, route_weights)

    return run
```
